32 devices in a mesh: dp: 8 (over y, x, core), tensor: 4 (over z).
Axes of the slice: x: 2, y: 2, z: 4, core: 2. Of those that a mesh axis runs over, the one named last changes fastest.
Arguments:
- block_input: bfloat16 [16384, 1024], P(('dp', 'tensor')), may hold values from -6 to 6
- ln1_gain: bfloat16 [1024], P(('dp', 'tensor')), may hold values from 0.5 to 1.5
- ln1_bias: bfloat16 [1024], P(('dp', 'tensor')), may hold values from -1.5 to 1.5
- w_query: bfloat16 [1024, 1024], P('dp', 'tensor'), may hold values from -0.1875 to 0.1875
- w_key: bfloat16 [1024, 1024], P('dp', 'tensor'), may hold values from -0.1875 to 0.1875
- w_value: bfloat16 [1024, 1024], P('dp', 'tensor'), may hold values from -0.1875 to 0.1875
- query_bias: bfloat16 [1024], P(('dp', 'tensor')), may hold values from -1.5 to 1.5
- value_bias: bfloat16 [1024], P(('dp', 'tensor')), may hold values from -1.5 to 1.5
- w_dense: bfloat16 [1024, 1024], P('tensor', 'dp'), may hold values from -0.5 to 0.5
- dense_bias: bfloat16 [1024], P(('dp', 'tensor')), may hold values from -1.5 to 1.5
- ln2_gain: bfloat16 [1024], P(('dp', 'tensor')), may hold values from 0.5 to 1.5
- ln2_bias: bfloat16 [1024], P(('dp', 'tensor')), may hold values from -1.5 to 1.5
- w_fc1: bfloat16 [1024, 4096], P('dp', 'tensor'), may hold values from -0.1875 to 0.1875
- fc1_bias: bfloat16 [4096], P(('dp', 'tensor')), may hold values from -1.5 to 1.5
- w_fc2: bfloat16 [4096, 1024], P('tensor', 'dp'), may hold values from -0.09375 to 0.09375
- fc2_bias: bfloat16 [1024], P(('dp', 'tensor')), may hold values from -1.5 to 1.5
- out_grad: bfloat16 [16384, 1024], P(('dp', 'tensor')), may hold values from -6 to 6
- doc_lengths: int32 [8, 8], P('dp'), may hold values from 1 to 512, 2048 in all within a row
Outputs:
- block_output: bfloat16 [16384, 1024], P(('dp', 'tensor'))
- input_grad: float32 [16384, 1024], P(('dp', 'tensor'))
- ln1_gain_grad: float32 [1024], P(('dp', 'tensor'))
- ln1_bias_grad: float32 [1024], P(('dp', 'tensor'))
- w_query_grad: float32 [1024, 1024], P('dp', 'tensor')
- w_key_grad: float32 [1024, 1024], P('dp', 'tensor')
- w_value_grad: float32 [1024, 1024], P('dp', 'tensor')
- query_bias_grad: float32 [1024], P(('dp', 'tensor'))
- value_bias_grad: float32 [1024], P(('dp', 'tensor'))
- w_dense_grad: float32 [1024, 1024], P('tensor', 'dp')
- dense_bias_grad: float32 [1024], P(('dp', 'tensor'))
- ln2_gain_grad: float32 [1024], P(('dp', 'tensor'))
- ln2_bias_grad: float32 [1024], P(('dp', 'tensor'))
- w_fc1_grad: float32 [1024, 4096], P('dp', 'tensor')
- fc1_bias_grad: float32 [4096], P(('dp', 'tensor'))
- w_fc2_grad: float32 [4096, 1024], P('tensor', 'dp')
- fc2_bias_grad: float32 [1024], P(('dp', 'tensor'))
The draws below stay inside these ranges and needn't reach their ends.
Inputs may be any that keep to these rules, and one draw needn't show every extreme that they name: `doc_lengths`: each packed row of 2048 tokens holds 8 documents whose lengths sum to 2048, the longest exactly 512.
All inputs are finite; a program needn't handle non-finite values.
Results may differ from the reference program's by a relative error of at most 0.018.
Values may be sent and summed in bfloat16 or wider, within the bound.
A program may use at most 192 MiB of HBM per device.

```python
import math
import jax
import jax.numpy as jnp
import numpy as np
from jax import lax

D = 1024
H = 16
HD = 64
FF = 4096
ROW = 2048
MOST = 512
DOCS = 8
GROUPS = 8
TOKENS = 16384


def levels(rng, shape, pieces, smallest, largest):
    def one(dim, shards_of):
        draws = jax.random.uniform(jax.random.fold_in(jax.random.fold_in(rng, 6), dim), (shards_of,), jnp.float32, smallest / len(pieces), largest / len(pieces))
        return jnp.repeat(jnp.exp(draws), shape[dim] // shards_of).reshape((-1,) + (1,) * (len(shape) - dim - 1))

    loudness = one(*pieces[0])
    for cut in pieces[1:]:
        loudness = loudness * one(*cut)
    return loudness


def profile(count, total, most, slope):
    portions = [(1 << 20) // math.isqrt(grade ** slope) + 1 for grade in range(2, count + 1)]
    surplus, given = total - most - (count - 1), [1] * (count - 1)
    while surplus > 0:
        candidates = [i for i in range(count - 1) if given[i] < most]
        whole, left = sum([portions[i] for i in candidates]), surplus
        for i in candidates:
            addition = min(most - given[i], max(1, left * portions[i] // whole), surplus)
            given[i] = given[i] + addition
            surplus = surplus - addition
    return np.array([most] + given)


def uneven_parts(stream_key, amount, total, limit, skew):
    if amount == 2:
        one = jax.random.randint(stream_key, (), max(1, total - limit), min(limit, total - 1) + 1)
        return jnp.stack([one, total - one])
    tallies = jnp.asarray(profile(amount, total, limit, skew), jnp.int32)
    pairs = (amount - 1) // 2
    giver, sink = tallies[1:1 + 2 * pairs:2], tallies[2:2 + 2 * pairs:2]
    room = jnp.minimum(giver - 1, limit - sink)
    passed = jax.random.randint(jax.random.fold_in(stream_key, 1), (pairs,), 0, 1 << 20) % (room + 1)
    tallies = tallies.at[1:1 + 2 * pairs:2].set(giver - passed).at[2:2 + 2 * pairs:2].set(sink + passed)
    return tallies[jax.random.permutation(jax.random.fold_in(stream_key, 2), amount)]


def normal_values(rng, extent, deviation, reach, cuts=(), held_as=jnp.bfloat16):
    values = jax.random.normal(rng, extent, jnp.float32) * deviation
    if len(cuts) > 0:
        values = levels(rng, extent, cuts, -0.22, 0.18) * values
    return jnp.clip(values, min=-reach, max=reach).astype(held_as)


def setup_inputs(seed: int = 0) -> dict:
    key_list = jax.random.split(jax.random.key(seed), 19)
    block_input = normal_values(key_list[0], (TOKENS, D), 1.0, 6.0, ((0, 32),))
    ln1_gain = jnp.clip(1.0 + 0.1 * jax.random.normal(key_list[1], (D,), jnp.float32), 0.5, 1.5).astype(jnp.bfloat16)
    ln1_bias = normal_values(key_list[2], (D,), 0.3, 1.5, ((0, 32),))
    w_query = normal_values(key_list[3], (D, D), D ** -0.5, 0.1875, ((0, 8), (1, 4)))
    w_key = normal_values(key_list[4], (D, D), D ** -0.5, 0.1875, ((0, 8), (1, 4)))
    w_value = normal_values(key_list[5], (D, D), D ** -0.5, 0.1875, ((0, 8), (1, 4)))
    query_bias = normal_values(key_list[6], (D,), 0.3, 1.5, ((0, 32),))
    value_bias = normal_values(key_list[7], (D,), 0.3, 1.5, ((0, 32),))
    w_dense = normal_values(key_list[8], (D, D), (D // 8) ** -0.5, 0.5, ((0, 4), (1, 8)))
    dense_bias = normal_values(key_list[9], (D,), 0.3, 1.5, ((0, 32),))
    ln2_gain = jnp.clip(1.0 + 0.1 * jax.random.normal(key_list[10], (D,), jnp.float32), 0.5, 1.5).astype(jnp.bfloat16)
    ln2_bias = normal_values(key_list[11], (D,), 0.3, 1.5, ((0, 32),))
    w_fc1 = normal_values(key_list[12], (D, FF), D ** -0.5, 0.1875, ((0, 8), (1, 4)))
    fc1_bias = normal_values(key_list[13], (FF,), 0.3, 1.5, ((0, 32),))
    w_fc2 = normal_values(key_list[14], (FF, D), FF ** -0.5, 0.09375, ((0, 4), (1, 8)))
    fc2_bias = normal_values(key_list[15], (D,), 0.3, 1.5, ((0, 32),))
    out_grad = normal_values(key_list[16], (TOKENS, D), 1.0, 6.0, ((0, 32),))
    doc_lengths = jax.vmap(lambda own: uneven_parts(own, DOCS, ROW, MOST, 2))(jax.random.split(key_list[17], GROUPS)).reshape((GROUPS, DOCS)).astype(jnp.int32)
    return dict(block_input=block_input, ln1_gain=ln1_gain, ln1_bias=ln1_bias, w_query=w_query, w_key=w_key, w_value=w_value, query_bias=query_bias, value_bias=value_bias, w_dense=w_dense, dense_bias=dense_bias, ln2_gain=ln2_gain, ln2_bias=ln2_bias, w_fc1=w_fc1, fc1_bias=fc1_bias, w_fc2=w_fc2, fc2_bias=fc2_bias, out_grad=out_grad, doc_lengths=doc_lengths)


@jax.custom_vjp
def low(v):
    return lax.optimization_barrier(v.astype(jnp.bfloat16)).astype(jnp.float32)

@jax.custom_vjp
def low_back(v):
    return v

def low_keep(v):
    return (low(v), None)

def low_pass(kept, grad):
    return (grad,)

def back_keep(v):
    return (v, None)

def back_low(kept, grad):
    return (low(grad),)
low.defvjp(low_keep, low_pass)
low_back.defvjp(back_keep, back_low)
EPSILON = 1e-05
MASK_VALUE = -1e+30

def layer_norm(values, gain, shift):
    center = lax.optimization_barrier(jnp.mean(values, axis=-1, keepdims=True))
    centered = values - center
    spread = lax.optimization_barrier(jnp.mean(centered * centered, axis=-1, keepdims=True))
    return centered * lax.rsqrt(spread + EPSILON) * gain + shift

def product(left, right):
    return jnp.dot(left, right, precision=lax.Precision.HIGHEST, preferred_element_type=jnp.float32)

def head_slopes():
    return 2.0 ** (-8.0 * (jnp.arange(H, dtype=jnp.float32) + 1.0) / H)

def attend_block(queries, keys_all, values_all, first_row, segment):
    block_rows = queries.shape[1]
    query_rows = first_row + jnp.arange(block_rows, dtype=jnp.int32)
    key_rows = jnp.arange(keys_all.shape[1], dtype=jnp.int32)
    query_segment = lax.dynamic_slice_in_dim(segment, first_row, block_rows)
    allowed = (key_rows[None, :] <= query_rows[:, None]) & (segment[None, :] == query_segment[:, None])
    distance = (query_rows[:, None] - key_rows[None, :]).astype(jnp.float32)
    raw = jnp.einsum('hqd,hkd->hqk', queries, keys_all, precision=lax.Precision.HIGHEST)
    scores = low_back(raw * HD ** (-0.5) - head_slopes()[:, None, None] * distance[None])
    scores = jnp.where(allowed[None], scores, MASK_VALUE)
    highest = lax.optimization_barrier(jnp.max(scores, axis=-1, keepdims=True))
    weights = jnp.exp(scores - highest)
    probs = low(weights / lax.optimization_barrier(jnp.sum(weights, axis=-1, keepdims=True)))
    return jnp.einsum('hqk,hkd->hqd', probs, values_all, precision=lax.Precision.HIGHEST)

def attention(queries, keys_all, values_all, segment):
    block_rows = min(512, ROW)
    blocks = ROW // block_rows
    query_blocks = queries.reshape(H, blocks, block_rows, HD).transpose(1, 0, 2, 3)
    firsts = jnp.arange(blocks, dtype=jnp.int32) * block_rows
    checked = jax.checkpoint(attend_block)
    outputs = lax.map(lambda packed: checked(packed[0], keys_all, values_all, packed[1], segment), (query_blocks, firsts))
    return outputs.transpose(0, 2, 1, 3).reshape(ROW, H * HD)

def to_heads(matrix):
    return matrix.reshape(ROW, H, HD).transpose(1, 0, 2)

def forward(params, inputs, segment):
    ln1_gain, ln1_bias, w_query, w_key, w_value, query_bias, value_bias, w_dense, dense_bias, ln2_gain, ln2_bias, w_fc1, fc1_bias, w_fc2, fc2_bias = params
    normed = low(layer_norm(inputs, ln1_gain, ln1_bias))
    query = low(low_back(product(normed, w_query) + query_bias))
    keys_all = low(low_back(product(normed, w_key)))
    values_all = low(low_back(product(normed, w_value) + value_bias))
    attended = attention(to_heads(query), to_heads(keys_all), to_heads(values_all), segment)
    attended = low(low_back(attended))
    mixed = inputs + low_back(product(attended, w_dense)) + dense_bias
    normed_mid = low(layer_norm(mixed, ln2_gain, ln2_bias))
    hidden = low_back(product(normed_mid, w_fc1) + fc1_bias)
    active = low(jax.nn.gelu(hidden, approximate=True))
    return mixed + low_back(product(active, w_fc2)) + fc2_bias

def reference(block_input, ln1_gain, ln1_bias, w_query, w_key, w_value, query_bias, value_bias, w_dense, dense_bias, ln2_gain, ln2_bias, w_fc1, fc1_bias, w_fc2, fc2_bias, out_grad, doc_lengths):
    params = tuple((param.astype(jnp.float32) for param in (ln1_gain, ln1_bias, w_query, w_key, w_value, query_bias, value_bias, w_dense, dense_bias, ln2_gain, ln2_bias, w_fc1, fc1_bias, w_fc2, fc2_bias)))
    inputs_all = block_input.astype(jnp.float32).reshape(GROUPS, ROW, D)
    cotangents = out_grad.astype(jnp.float32).reshape(GROUPS, ROW, D)

    def group_step(summed, packed):
        inputs, cotangent, lengths = packed
        doc_ends = jnp.cumsum(lengths)
        places = jnp.arange(ROW, dtype=jnp.int32)
        segment = lax.optimization_barrier(jnp.sum((places[:, None] >= doc_ends[None, :]).astype(jnp.int32), axis=1))
        output, puller = jax.vjp(lambda weights, source: forward(weights, source, segment), params, inputs)
        param_grads, input_grads = puller(cotangent)
        summed = jax.tree.map(lambda left, right: left + right, summed, param_grads)
        return (summed, (output.astype(jnp.bfloat16), input_grads))
    zeroes = tuple((jnp.zeros_like(param) for param in params))
    summed, (outputs, input_grads) = lax.scan(group_step, zeroes, (inputs_all, cotangents, doc_lengths))
    grad_ln1_gain, grad_ln1_bias, grad_query, grad_key, grad_value, grad_query_bias, grad_value_bias, grad_dense, grad_dense_bias, grad_ln2_gain, grad_ln2_bias, grad_fc1, grad_fc1_bias, grad_fc2, grad_fc2_bias = summed
    return (outputs.reshape(TOKENS, D), input_grads.reshape(TOKENS, D), grad_ln1_gain, grad_ln1_bias, grad_query, grad_key, grad_value, grad_query_bias, grad_value_bias, grad_dense, grad_dense_bias, grad_ln2_gain, grad_ln2_bias, grad_fc1, grad_fc1_bias, grad_fc2, grad_fc2_bias)
```

```python
import functools

import jax
import jax.numpy as jnp
from jax import lax
from jax.experimental import pallas as pl
from jax.experimental.pallas import tpu as pltpu
from jax.sharding import PartitionSpec as P

H = 16
HD = 64
MOST = 512
BLOCK = 256

EPSILON = 1e-05
EXCLUDED = 1e30
BF = jnp.bfloat16
F32 = jnp.float32


def norm_parts(values):
    center = jnp.mean(values, axis=-1, keepdims=True)
    centered = values - center
    spread = jnp.mean(centered * centered, axis=-1, keepdims=True)
    inverse = lax.rsqrt(spread + EPSILON)
    return centered * inverse, inverse


def norm_pull(grad, unit, inverse, gain):
    scaled = grad * gain
    mean_one = jnp.mean(scaled, axis=-1, keepdims=True)
    mean_two = jnp.mean(scaled * unit, axis=-1, keepdims=True)
    return inverse * (scaled - mean_one - unit * mean_two)


def gelu_tanh(values):
    return jax.nn.gelu(values, approximate=True)


def dot(left, right, left_dim=1, right_dim=0):
    return lax.dot_general(
        left, right, (((left_dim,), (right_dim,)), ((), ())), preferred_element_type=F32
    )


def slope_of(head):
    return jnp.exp2(-0.5 * (head.astype(F32) + 1.0))


def attend_kernel(q_ref, k_ref, v_ref, far_ref, o_ref, lse_ref):
    pair = pl.program_id(0)
    rows = q_ref.shape[0]
    window = BLOCK + MOST
    for place in range(2):
        slope = slope_of(jnp.full((1, 1), pair * 2 + place, jnp.int32))
        lanes = slice(place * HD, (place + 1) * HD)
        for block in range(rows // BLOCK):
            first = block * BLOCK
            mine = slice(first, first + BLOCK)
            keys = slice(first, first + window)
            scores = dot(q_ref[mine, lanes], k_ref[keys, lanes], 1, 1)
            scores = scores - slope * far_ref[mine, keys]
            highest = jnp.max(scores, axis=-1, keepdims=True)
            weights = jnp.exp(scores - highest)
            mass = jnp.sum(weights, axis=-1, keepdims=True)
            result = dot((weights * (1.0 / mass)).astype(BF), v_ref[keys, lanes])
            o_ref[mine, lanes] = result.astype(BF)
            lse_ref[place, mine, :] = highest + jnp.log(mass)


def attend_back_kernel(
    q_ref, k_ref, v_ref, far_ref, g_ref, lse_ref, dq_ref, dk_ref, dv_ref, dk_sum, dv_sum
):
    pair = pl.program_id(0)
    rows = q_ref.shape[0]
    window = BLOCK + MOST
    dk_sum[...] = jnp.zeros_like(dk_sum)
    dv_sum[...] = jnp.zeros_like(dv_sum)
    for place in range(2):
        slope = slope_of(jnp.full((1, 1), pair * 2 + place, jnp.int32))
        lanes = slice(place * HD, (place + 1) * HD)
        for block in range(rows // BLOCK):
            first = block * BLOCK
            mine = slice(first, first + BLOCK)
            keys = slice(first, first + window)
            query = q_ref[mine, lanes]
            key = k_ref[keys, lanes]
            grad = g_ref[mine, lanes]
            scores = dot(query, key, 1, 1) - slope * far_ref[mine, keys]
            probs = jnp.exp(scores - lse_ref[place, mine, :])
            grad_probs = dot(grad, v_ref[keys, lanes], 1, 1)
            weighted = jnp.sum(probs * grad_probs, axis=-1, keepdims=True)
            grad_scores = (probs * (grad_probs - weighted)).astype(BF)
            dq_ref[mine, lanes] = (dot(grad_scores, key) * HD ** (-0.5)).astype(BF)
            dk_sum[keys, lanes] += dot(grad_scores, query, 0, 0)
            dv_sum[keys, lanes] += dot(probs.astype(BF), grad, 0, 0)
    dk_ref[...] = dk_sum[...].astype(BF)
    dv_ref[...] = dv_sum[...].astype(BF)


def attend(query, keys, values, far):
    rows, width = query.shape
    reach = keys.shape[0]
    pairs = width // (2 * HD)
    column = pl.BlockSpec((rows, 2 * HD), lambda i: (0, i))
    tall = pl.BlockSpec((reach, 2 * HD), lambda i: (0, i))
    whole = pl.BlockSpec((rows, reach), lambda i: (0, 0))
    return pl.pallas_call(
        attend_kernel,
        grid=(pairs,),
        in_specs=[column, tall, tall, whole],
        out_specs=[column, pl.BlockSpec((2, rows, 1), lambda i: (i, 0, 0))],
        out_shape=[
            jax.ShapeDtypeStruct((rows, width), BF),
            jax.ShapeDtypeStruct((2 * pairs, rows, 1), F32),
        ],
        compiler_params=pltpu.CompilerParams(vmem_limit_bytes=40 * 1024 * 1024),
        cost_estimate=pl.CostEstimate(
            flops=40_000_000_000, bytes_accessed=20_000_000, transcendentals=6_000_000
        ),
    )(query, keys, values, far)


def attend_back(query, keys, values, far, grad, lse):
    rows, width = query.shape
    reach = keys.shape[0]
    pairs = width // (2 * HD)
    column = pl.BlockSpec((rows, 2 * HD), lambda i: (0, i))
    tall = pl.BlockSpec((reach, 2 * HD), lambda i: (0, i))
    whole = pl.BlockSpec((rows, reach), lambda i: (0, 0))
    mass = pl.BlockSpec((2, rows, 1), lambda i: (i, 0, 0))
    return pl.pallas_call(
        attend_back_kernel,
        grid=(pairs,),
        in_specs=[column, tall, tall, whole, column, mass],
        out_specs=[column, tall, tall],
        out_shape=[
            jax.ShapeDtypeStruct((rows, width), BF),
            jax.ShapeDtypeStruct((reach, width), BF),
            jax.ShapeDtypeStruct((reach, width), BF),
        ],
        scratch_shapes=[pltpu.VMEM((reach, 2 * HD), F32), pltpu.VMEM((reach, 2 * HD), F32)],
        compiler_params=pltpu.CompilerParams(vmem_limit_bytes=40 * 1024 * 1024),
        cost_estimate=pl.CostEstimate(
            flops=80_000_000_000, bytes_accessed=30_000_000, transcendentals=6_000_000
        ),
    )(query, keys, values, far, grad, lse)


def gather_plane(parts):
    count = len(parts)
    rows, width = parts[0].shape
    packed = jnp.concatenate(parts, axis=1)
    lines = lax.all_gather(packed, "tensor", axis=0, tiled=False)
    tensor = lines.shape[0]
    lines = lines.reshape(tensor, rows, count, width).transpose(1, 2, 0, 3)
    lines = lines.reshape(rows, count * tensor * width)
    return lax.all_gather(lines, "dp", axis=0, tiled=True)


def scatter_line(summed, count):
    rows = summed.shape[0]
    tensor = lax.axis_size("tensor")
    split = summed.reshape(rows, count, tensor, -1).transpose(2, 0, 1, 3)
    own = lax.psum_scatter(split, "tensor", scatter_dimension=0, tiled=False)
    return [own[:, i, :].astype(F32) for i in range(count)]


def scatter_plane(grads):
    return lax.psum_scatter(grads, "dp", scatter_dimension=0, tiled=True)


def per_device(
    block_input,
    ln1_gain,
    ln1_bias,
    w_query,
    w_key,
    w_value,
    query_bias,
    value_bias,
    w_dense,
    dense_bias,
    ln2_gain,
    ln2_bias,
    w_fc1,
    fc1_bias,
    w_fc2,
    fc2_bias,
    out_grad,
    doc_lengths,
):
    rows, width = block_input.shape
    dp = lax.axis_size("dp")
    tensor = lax.axis_size("tensor")
    place = lax.axis_index("tensor")
    onward = [(i, i + 1) for i in range(tensor - 1)]
    backward = [(i + 1, i) for i in range(tensor - 1)]

    halo = lax.ppermute(block_input, "tensor", onward)

    small = jnp.concatenate(
        [
            ln1_gain,
            ln1_bias,
            query_bias,
            value_bias,
            dense_bias,
            ln2_gain,
            ln2_bias,
            fc1_bias,
            fc2_bias,
        ]
    )
    small_width = small.shape[0]
    piece = ln1_gain.shape[0]
    hidden_piece = fc1_bias.shape[0]
    padded = -(-small_width // 128) * 128
    small = jnp.pad(small, (0, padded - small_width))[None]
    vectors = lax.all_gather(small, ("dp", "tensor"), axis=0, tiled=True).astype(F32)
    pieces = [piece] * 7 + [hidden_piece, piece]
    starts = [sum(pieces[:i]) for i in range(len(pieces))]
    (
        gain_first,
        shift_first,
        query_shift,
        value_shift,
        dense_shift,
        gain_second,
        shift_second,
        hidden_shift,
        output_shift,
    ) = [vectors[:, s : s + n].reshape(-1) for s, n in zip(starts, pieces)]

    attn_weights = gather_plane([w_query, w_key, w_value, w_dense.T])
    ffn_first = gather_plane([w_fc1])
    ffn_second = gather_plane([w_fc2.T])
    qkv_weights = attn_weights[:, : 3 * width]
    dense_t = attn_weights[:, 3 * width :]

    extended = jnp.concatenate([halo, block_input], axis=0).astype(F32)
    unit_first, inverse_first = norm_parts(extended)
    normed_in = (unit_first * gain_first + shift_first).astype(BF)
    qkv_shift = jnp.concatenate([query_shift, jnp.zeros_like(query_shift), value_shift])
    query = (
        (dot(normed_in[rows:], qkv_weights[:, :width]) + query_shift).astype(BF) * HD ** (-0.5)
    ).astype(BF)
    kv = (dot(normed_in, qkv_weights[:, width:]) + qkv_shift[width:]).astype(BF)
    keys, values = kv[:, :width], kv[:, width:]

    doc_ends = jnp.cumsum(doc_lengths[0])
    key_rows = place * rows - rows + jnp.arange(2 * rows, dtype=jnp.int32)
    segment = jnp.sum((key_rows[:, None] >= doc_ends[None, :]).astype(jnp.int32), axis=1)
    segment = jnp.where(key_rows < 0, -1, segment)
    query_rows = key_rows[rows:]
    distance = query_rows[:, None] - key_rows[None, :]
    allowed = (distance >= 0) & (segment[rows:, None] == segment[None, :])
    far = jnp.where(allowed, distance.astype(F32), EXCLUDED)

    attended, lse = attend(query, keys, values, far)

    rows_in = block_input.astype(F32)
    mixed = rows_in + dot(attended, dense_t, 1, 1) + dense_shift
    unit_second, inverse_second = norm_parts(mixed)
    normed_mid = (unit_second * gain_second + shift_second).astype(BF)
    pre_act = dot(normed_mid, ffn_first) + hidden_shift
    active, gelu_pull = jax.vjp(gelu_tanh, pre_act)
    active = active.astype(BF)
    block_output = (mixed + dot(active, ffn_second, 1, 1) + output_shift).astype(BF)

    grad_output = out_grad.astype(F32)
    grad_fc2 = dot(out_grad, active, 0, 0).astype(BF)
    fc2_sum = scatter_plane(grad_fc2)
    grad_active = dot(out_grad, ffn_second)
    grad_pre = gelu_pull(grad_active)[0].astype(BF)
    grad_fc1 = dot(normed_mid, grad_pre, 0, 0).astype(BF)
    fc1_sum = scatter_plane(grad_fc1)
    grad_mid = dot(grad_pre, ffn_first, 1, 1)
    grad_mixed = grad_output + norm_pull(grad_mid, unit_second, inverse_second, gain_second)
    grad_attn = grad_mixed.astype(BF)
    grad_dense = dot(grad_attn, attended, 0, 0).astype(BF)
    grad_attended = dot(grad_attn, dense_t).astype(BF)

    grad_query, grad_keys, grad_values = attend_back(query, keys, values, far, grad_attended, lse)
    grad_kv = jnp.concatenate([grad_keys, grad_values], axis=1)
    grad_in_kv = dot(grad_kv, qkv_weights[:, width:], 1, 1)
    grad_in_own = grad_in_kv[rows:] + dot(grad_query, qkv_weights[:, :width], 1, 1)
    grad_in_halo = grad_in_kv[:rows]
    returned = lax.ppermute(grad_in_halo.astype(BF), "tensor", backward)

    own_unit = unit_first[rows:]
    halo_unit = unit_first[:rows]
    small_grads = [
        jnp.sum(grad_in_own * own_unit, axis=0) + jnp.sum(grad_in_halo * halo_unit, axis=0),
        jnp.sum(grad_in_own, axis=0) + jnp.sum(grad_in_halo, axis=0),
        jnp.sum(grad_query.astype(F32), axis=0),
        jnp.sum(grad_values.astype(F32), axis=0),
        jnp.sum(grad_mixed, axis=0),
        jnp.sum(grad_mid * unit_second, axis=0),
        jnp.sum(grad_mid, axis=0),
        jnp.sum(grad_pre.astype(F32), axis=0),
        jnp.sum(grad_output, axis=0),
    ]
    shares = [g.reshape(dp, tensor, -1) for g in small_grads]
    shares = jnp.concatenate(shares, axis=2)
    shares = jnp.pad(shares, ((0, 0), (0, 0), (0, padded - small_width)))
    block_width = width // dp
    lanes = 128 * -(-(tensor * padded) // (128 * block_width))
    shares = shares.reshape(dp, tensor * padded)
    shares = jnp.pad(shares, ((0, 0), (0, block_width * lanes - tensor * padded)))
    shares = shares.reshape(width, lanes).astype(BF)

    grad_q_w = dot(normed_in[rows:], grad_query, 0, 0).astype(BF)
    grad_kv_w = dot(normed_in, grad_kv, 0, 0).astype(BF)
    last_sum = scatter_plane(jnp.concatenate([grad_q_w, grad_kv_w, grad_dense, shares], axis=1))

    grad_normed = grad_in_own + returned.astype(F32)
    input_grad = grad_mixed + norm_pull(grad_normed, own_unit, inverse_first[rows:], gain_first)

    (fc2_own,) = scatter_line(fc2_sum, 1)
    (fc1_own,) = scatter_line(fc1_sum, 1)
    split = last_sum[:, : 4 * width].reshape(block_width, 4, tensor, -1).transpose(2, 0, 1, 3)
    split = split.reshape(tensor, block_width, -1)
    small_sum = last_sum[:, 4 * width :].reshape(-1)[: tensor * padded].reshape(tensor, padded)
    extra = split.shape[2]
    small_rows = -(-padded // extra)
    small_sum = jnp.pad(small_sum, ((0, 0), (0, small_rows * extra - padded)))
    split = jnp.concatenate([split, small_sum.reshape(tensor, small_rows, extra)], axis=1)
    own = lax.psum_scatter(split, "tensor", scatter_dimension=0, tiled=False)
    own_small = own[block_width:].reshape(-1).astype(F32)
    own = own[:block_width].reshape(block_width, 4, -1).astype(F32)
    out_small = [own_small[s : s + n] for s, n in zip(starts, pieces)]
    return (
        block_output,
        input_grad,
        out_small[0],
        out_small[1],
        own[:, 0],
        own[:, 1],
        own[:, 2],
        out_small[2],
        out_small[3],
        own[:, 3].T,
        out_small[4],
        out_small[5],
        out_small[6],
        fc1_own,
        out_small[7],
        fc2_own.T,
        out_small[8],
    )


def solution(mesh):
    every = P(("dp", "tensor"))
    tokens = P(("dp", "tensor"), None)
    row_cut = P("dp", "tensor")
    col_cut = P("tensor", "dp")
    return jax.shard_map(
        per_device,
        mesh=mesh,
        in_specs=(
            tokens,
            every,
            every,
            row_cut,
            row_cut,
            row_cut,
            every,
            every,
            col_cut,
            every,
            every,
            every,
            row_cut,
            every,
            col_cut,
            every,
            tokens,
            P("dp", None),
        ),
        out_specs=(
            tokens,
            tokens,
            every,
            every,
            row_cut,
            row_cut,
            row_cut,
            every,
            every,
            col_cut,
            every,
            every,
            every,
            row_cut,
            every,
            col_cut,
            every,
        ),
        check_vma=False,
    )
```

```python
import functools

import jax
import jax.numpy as jnp
from jax import lax
from jax.experimental import pallas as pl
from jax.experimental.pallas import tpu as pltpu
from jax.sharding import PartitionSpec as P

H = 16
HD = 64
MOST = 512
BLOCK = 256

EPSILON = 1e-05
EXCLUDED = 1e30
BF = jnp.bfloat16
F32 = jnp.float32


def norm_parts(values):
    center = jnp.mean(values, axis=-1, keepdims=True)
    centered = values - center
    spread = jnp.mean(centered * centered, axis=-1, keepdims=True)
    inverse = lax.rsqrt(spread + EPSILON)
    return centered * inverse, inverse


def norm_pull(grad, unit, inverse, gain):
    scaled = grad * gain
    mean_one = jnp.mean(scaled, axis=-1, keepdims=True)
    mean_two = jnp.mean(scaled * unit, axis=-1, keepdims=True)
    return inverse * (scaled - mean_one - unit * mean_two)


def gelu_tanh(values):
    return jax.nn.gelu(values, approximate=True)


def dot(left, right, left_dim=1, right_dim=0):
    return lax.dot_general(
        left, right, (((left_dim,), (right_dim,)), ((), ())), preferred_element_type=F32
    )


def slope_of(head):
    return jnp.exp2(-0.5 * (head.astype(F32) + 1.0))


def attend_kernel(q_ref, k_ref, v_ref, far_ref, o_ref, lse_ref):
    pair = pl.program_id(0)
    rows = q_ref.shape[0]
    window = BLOCK + MOST
    for place in range(2):
        slope = slope_of(jnp.full((1, 1), pair * 2 + place, jnp.int32))
        lanes = slice(place * HD, (place + 1) * HD)
        for block in range(rows // BLOCK):
            first = block * BLOCK
            mine = slice(first, first + BLOCK)
            keys = slice(first, first + window)
            scores = dot(q_ref[mine, lanes], k_ref[keys, lanes], 1, 1)
            scores = scores - slope * far_ref[mine, keys]
            highest = jnp.max(scores, axis=-1, keepdims=True)
            weights = jnp.exp(scores - highest)
            mass = jnp.sum(weights, axis=-1, keepdims=True)
            result = dot((weights * (1.0 / mass)).astype(BF), v_ref[keys, lanes])
            o_ref[mine, lanes] = result.astype(BF)
            lse_ref[place, mine, :] = highest + jnp.log(mass)


def attend_back_kernel(
    q_ref, k_ref, v_ref, far_ref, g_ref, lse_ref, dq_ref, dk_ref, dv_ref, dk_sum, dv_sum
):
    pair = pl.program_id(0)
    rows = q_ref.shape[0]
    window = BLOCK + MOST
    dk_sum[...] = jnp.zeros_like(dk_sum)
    dv_sum[...] = jnp.zeros_like(dv_sum)
    for place in range(2):
        slope = slope_of(jnp.full((1, 1), pair * 2 + place, jnp.int32))
        lanes = slice(place * HD, (place + 1) * HD)
        for block in range(rows // BLOCK):
            first = block * BLOCK
            mine = slice(first, first + BLOCK)
            keys = slice(first, first + window)
            query = q_ref[mine, lanes]
            key = k_ref[keys, lanes]
            grad = g_ref[mine, lanes]
            scores = dot(query, key, 1, 1) - slope * far_ref[mine, keys]
            probs = jnp.exp(scores - lse_ref[place, mine, :])
            grad_probs = dot(grad, v_ref[keys, lanes], 1, 1)
            weighted = jnp.sum(probs * grad_probs, axis=-1, keepdims=True)
            grad_scores = (probs * (grad_probs - weighted)).astype(BF)
            dq_ref[mine, lanes] = (dot(grad_scores, key) * HD ** (-0.5)).astype(BF)
            dk_sum[keys, lanes] += dot(grad_scores, query, 0, 0)
            dv_sum[keys, lanes] += dot(probs.astype(BF), grad, 0, 0)
    dk_ref[...] = dk_sum[...].astype(BF)
    dv_ref[...] = dv_sum[...].astype(BF)


def attend(query, keys, values, far):
    rows, width = query.shape
    reach = keys.shape[0]
    pairs = width // (2 * HD)
    column = pl.BlockSpec((rows, 2 * HD), lambda i: (0, i))
    tall = pl.BlockSpec((reach, 2 * HD), lambda i: (0, i))
    whole = pl.BlockSpec((rows, reach), lambda i: (0, 0))
    return pl.pallas_call(
        attend_kernel,
        grid=(pairs,),
        in_specs=[column, tall, tall, whole],
        out_specs=[column, pl.BlockSpec((2, rows, 1), lambda i: (i, 0, 0))],
        out_shape=[
            jax.ShapeDtypeStruct((rows, width), BF),
            jax.ShapeDtypeStruct((2 * pairs, rows, 1), F32),
        ],
        compiler_params=pltpu.CompilerParams(vmem_limit_bytes=40 * 1024 * 1024),
        cost_estimate=pl.CostEstimate(
            flops=40_000_000_000, bytes_accessed=20_000_000, transcendentals=6_000_000
        ),
    )(query, keys, values, far)


def attend_back(query, keys, values, far, grad, lse):
    rows, width = query.shape
    reach = keys.shape[0]
    pairs = width // (2 * HD)
    column = pl.BlockSpec((rows, 2 * HD), lambda i: (0, i))
    tall = pl.BlockSpec((reach, 2 * HD), lambda i: (0, i))
    whole = pl.BlockSpec((rows, reach), lambda i: (0, 0))
    mass = pl.BlockSpec((2, rows, 1), lambda i: (i, 0, 0))
    return pl.pallas_call(
        attend_back_kernel,
        grid=(pairs,),
        in_specs=[column, tall, tall, whole, column, mass],
        out_specs=[column, tall, tall],
        out_shape=[
            jax.ShapeDtypeStruct((rows, width), BF),
            jax.ShapeDtypeStruct((reach, width), BF),
            jax.ShapeDtypeStruct((reach, width), BF),
        ],
        scratch_shapes=[pltpu.VMEM((reach, 2 * HD), F32), pltpu.VMEM((reach, 2 * HD), F32)],
        compiler_params=pltpu.CompilerParams(vmem_limit_bytes=40 * 1024 * 1024),
        cost_estimate=pl.CostEstimate(
            flops=80_000_000_000, bytes_accessed=30_000_000, transcendentals=6_000_000
        ),
    )(query, keys, values, far, grad, lse)


def shift_by(value, step):
    size = lax.axis_size("tensor")
    return lax.ppermute(value, "tensor", [(i, (i + step) % size) for i in range(size)])


def gather_line(value):
    size = lax.axis_size("tensor")
    place = lax.axis_index("tensor")
    arrived = [value] + [shift_by(value, step) for step in range(1, size)]
    ordered = jnp.stack(arrived[::-1] * 2)
    return lax.dynamic_slice_in_dim(ordered, (2 * size - 1 - place) % size, size)


def sum_line(split):
    size = lax.axis_size("tensor")
    place = lax.axis_index("tensor")
    total = lax.dynamic_index_in_dim(split, place, keepdims=False).astype(F32)
    for step in range(1, size):
        sent = lax.dynamic_index_in_dim(split, (place + step) % size, keepdims=False)
        total = total + shift_by(sent, step).astype(F32)
    return total


def merge_line(lines, count):
    tensor, rows, columns = lines.shape
    lines = lines.reshape(tensor, rows, count, columns // count).transpose(1, 2, 0, 3)
    return lines.reshape(rows, tensor * columns)


def after(arrived, value):
    token = arrived[(0,) * arrived.ndim]
    return jnp.where(jnp.isnan(token), jnp.zeros_like(value), value)


def gather_rows(lines):
    return lax.all_gather(lines, "dp", axis=0, tiled=True)


def scatter_line(summed, count):
    rows = summed.shape[0]
    tensor = lax.axis_size("tensor")
    split = summed.reshape(rows, count, tensor, -1).transpose(2, 0, 1, 3)
    own = sum_line(split)
    return [own[:, i, :] for i in range(count)]


def scatter_plane(grads):
    return lax.psum_scatter(grads, "dp", scatter_dimension=0, tiled=True)


def per_device(
    block_input,
    ln1_gain,
    ln1_bias,
    w_query,
    w_key,
    w_value,
    query_bias,
    value_bias,
    w_dense,
    dense_bias,
    ln2_gain,
    ln2_bias,
    w_fc1,
    fc1_bias,
    w_fc2,
    fc2_bias,
    out_grad,
    doc_lengths,
):
    rows, width = block_input.shape
    dp = lax.axis_size("dp")
    tensor = lax.axis_size("tensor")
    place = lax.axis_index("tensor")
    onward = [(i, i + 1) for i in range(tensor - 1)]
    backward = [(i + 1, i) for i in range(tensor - 1)]

    small = jnp.concatenate(
        [
            ln1_gain,
            ln1_bias,
            query_bias,
            value_bias,
            dense_bias,
            ln2_gain,
            ln2_bias,
            fc1_bias,
            fc2_bias,
        ]
    )
    small_width = small.shape[0]
    piece = ln1_gain.shape[0]
    hidden_piece = fc1_bias.shape[0]
    padded = -(-small_width // 128) * 128

    attn_local = jnp.concatenate([w_query, w_key, w_value, w_dense.T], axis=1)
    block_width, attn_width = attn_local.shape
    lanes = 128 * -(-(tensor * padded) // (128 * block_width))
    small = jnp.pad(small, (0, 16 * attn_width - small_width)).reshape(16, attn_width)
    first_lines = lax.all_gather(
        jnp.concatenate([attn_local, small], axis=0), "tensor", axis=0, tiled=False
    )
    small_lines = first_lines[:, block_width:].reshape(tensor, -1)[:, :padded].reshape(-1)
    small_lines = jnp.pad(small_lines, (0, block_width * lanes - tensor * padded))
    attn_lines = jnp.concatenate(
        [merge_line(first_lines[:, :block_width], 4), small_lines.reshape(block_width, lanes)],
        axis=1,
    )
    attn_weights = gather_rows(attn_lines)

    halo = lax.ppermute(after(first_lines, block_input), "tensor", onward)
    fc1_lines = merge_line(gather_line(after(first_lines, w_fc1)), 1)
    fc2_lines = merge_line(gather_line(after(first_lines, w_fc2.T)), 1)
    ffn_first = gather_rows(after(attn_weights, fc1_lines))
    ffn_second = gather_rows(after(ffn_first, fc2_lines))

    vectors = attn_weights[:, 4 * width :].reshape(dp, block_width * lanes)[:, : tensor * padded]
    vectors = vectors.reshape(dp * tensor, padded).astype(F32)
    pieces = [piece] * 7 + [hidden_piece, piece]
    starts = [sum(pieces[:i]) for i in range(len(pieces))]
    (
        gain_first,
        shift_first,
        query_shift,
        value_shift,
        dense_shift,
        gain_second,
        shift_second,
        hidden_shift,
        output_shift,
    ) = [vectors[:, s : s + n].reshape(-1) for s, n in zip(starts, pieces)]

    qkv_weights = attn_weights[:, : 3 * width]
    dense_t = attn_weights[:, 3 * width : 4 * width]

    extended = jnp.concatenate([halo, block_input], axis=0).astype(F32)
    unit_first, inverse_first = norm_parts(extended)
    normed_in = (unit_first * gain_first + shift_first).astype(BF)
    qkv_shift = jnp.concatenate([query_shift, jnp.zeros_like(query_shift), value_shift])
    query = (
        (dot(normed_in[rows:], qkv_weights[:, :width]) + query_shift).astype(BF) * HD ** (-0.5)
    ).astype(BF)
    kv = (dot(normed_in, qkv_weights[:, width:]) + qkv_shift[width:]).astype(BF)
    keys, values = kv[:, :width], kv[:, width:]

    doc_ends = jnp.cumsum(doc_lengths[0])
    key_rows = place * rows - rows + jnp.arange(2 * rows, dtype=jnp.int32)
    segment = jnp.sum((key_rows[:, None] >= doc_ends[None, :]).astype(jnp.int32), axis=1)
    segment = jnp.where(key_rows < 0, -1, segment)
    query_rows = key_rows[rows:]
    distance = query_rows[:, None] - key_rows[None, :]
    allowed = (distance >= 0) & (segment[rows:, None] == segment[None, :])
    far = jnp.where(allowed, distance.astype(F32), EXCLUDED)

    attended, lse = attend(query, keys, values, far)

    rows_in = block_input.astype(F32)
    mixed = rows_in + dot(attended, dense_t, 1, 1) + dense_shift
    unit_second, inverse_second = norm_parts(mixed)
    normed_mid = (unit_second * gain_second + shift_second).astype(BF)
    pre_act = dot(normed_mid, ffn_first) + hidden_shift
    active, gelu_pull = jax.vjp(gelu_tanh, pre_act)
    active = active.astype(BF)
    block_output = (mixed + dot(active, ffn_second, 1, 1) + output_shift).astype(BF)

    grad_output = out_grad.astype(F32)
    grad_fc2 = dot(out_grad, active, 0, 0).astype(BF)
    fc2_sum = scatter_plane(grad_fc2)
    grad_active = dot(out_grad, ffn_second)
    grad_pre = gelu_pull(grad_active)[0].astype(BF)
    grad_fc1 = dot(normed_mid, grad_pre, 0, 0).astype(BF)
    fc1_sum = scatter_plane(grad_fc1)
    grad_mid = dot(grad_pre, ffn_first, 1, 1)
    grad_mixed = grad_output + norm_pull(grad_mid, unit_second, inverse_second, gain_second)
    grad_attn = grad_mixed.astype(BF)
    grad_dense = dot(grad_attn, attended, 0, 0).astype(BF)
    grad_attended = dot(grad_attn, dense_t).astype(BF)

    grad_query, grad_keys, grad_values = attend_back(query, keys, values, far, grad_attended, lse)
    grad_kv = jnp.concatenate([grad_keys, grad_values], axis=1)
    grad_in_kv = dot(grad_kv, qkv_weights[:, width:], 1, 1)
    grad_in_own = grad_in_kv[rows:] + dot(grad_query, qkv_weights[:, :width], 1, 1)
    grad_in_halo = grad_in_kv[:rows]
    returned = lax.ppermute(grad_in_halo.astype(BF), "tensor", backward)

    own_unit = unit_first[rows:]
    halo_unit = unit_first[:rows]
    small_grads = [
        jnp.sum(grad_in_own * own_unit, axis=0) + jnp.sum(grad_in_halo * halo_unit, axis=0),
        jnp.sum(grad_in_own, axis=0) + jnp.sum(grad_in_halo, axis=0),
        jnp.sum(grad_query.astype(F32), axis=0),
        jnp.sum(grad_values.astype(F32), axis=0),
        jnp.sum(grad_mixed, axis=0),
        jnp.sum(grad_mid * unit_second, axis=0),
        jnp.sum(grad_mid, axis=0),
        jnp.sum(grad_pre.astype(F32), axis=0),
        jnp.sum(grad_output, axis=0),
    ]
    shares = [g.reshape(dp, tensor, -1) for g in small_grads]
    shares = jnp.concatenate(shares, axis=2)
    shares = jnp.pad(shares, ((0, 0), (0, 0), (0, padded - small_width)))
    shares = shares.reshape(dp, tensor * padded)
    shares = jnp.pad(shares, ((0, 0), (0, block_width * lanes - tensor * padded)))
    shares = shares.reshape(width, lanes).astype(BF)

    grad_q_w = dot(normed_in[rows:], grad_query, 0, 0).astype(BF)
    grad_kv_w = dot(normed_in, grad_kv, 0, 0).astype(BF)
    last_sum = scatter_plane(jnp.concatenate([grad_q_w, grad_kv_w, grad_dense, shares], axis=1))

    grad_normed = grad_in_own + returned.astype(F32)
    input_grad = grad_mixed + norm_pull(grad_normed, own_unit, inverse_first[rows:], gain_first)

    (fc2_own,) = scatter_line(fc2_sum, 1)
    (fc1_own,) = scatter_line(fc1_sum, 1)
    split = last_sum[:, : 4 * width].reshape(block_width, 4, tensor, -1).transpose(2, 0, 1, 3)
    split = split.reshape(tensor, block_width, -1)
    small_sum = last_sum[:, 4 * width :].reshape(-1)[: tensor * padded].reshape(tensor, padded)
    extra = split.shape[2]
    small_rows = 16 * -(-padded // (16 * extra))
    small_sum = jnp.pad(small_sum, ((0, 0), (0, small_rows * extra - padded)))
    split = jnp.concatenate([split, small_sum.reshape(tensor, small_rows, extra)], axis=1)
    own = lax.psum_scatter(split, "tensor", scatter_dimension=0, tiled=False)
    own_small = own[block_width:].reshape(-1).astype(F32)
    own = own[:block_width].reshape(block_width, 4, -1).astype(F32)
    out_small = [own_small[s : s + n] for s, n in zip(starts, pieces)]
    return (
        block_output,
        input_grad,
        out_small[0],
        out_small[1],
        own[:, 0],
        own[:, 1],
        own[:, 2],
        out_small[2],
        out_small[3],
        own[:, 3].T,
        out_small[4],
        out_small[5],
        out_small[6],
        fc1_own,
        out_small[7],
        fc2_own.T,
        out_small[8],
    )


def solution(mesh):
    every = P(("dp", "tensor"))
    tokens = P(("dp", "tensor"), None)
    row_cut = P("dp", "tensor")
    col_cut = P("tensor", "dp")
    return jax.shard_map(
        per_device,
        mesh=mesh,
        in_specs=(
            tokens,
            every,
            every,
            row_cut,
            row_cut,
            row_cut,
            every,
            every,
            col_cut,
            every,
            every,
            every,
            row_cut,
            every,
            col_cut,
            every,
            tokens,
            P("dp", None),
        ),
        out_specs=(
            tokens,
            tokens,
            every,
            every,
            row_cut,
            row_cut,
            row_cut,
            every,
            every,
            col_cut,
            every,
            every,
            every,
            row_cut,
            every,
            col_cut,
            every,
        ),
        check_vma=False,
    )
```
